32 devices in a mesh: dp: 4 (over y, x), tensor: 8 (over z, core).
Axes of the slice: x: 2, y: 2, z: 4, core: 2. Of those that a mesh axis runs over, the one named last changes fastest.
Arguments:
- token_ids: int32 [512], replicated, may hold values from 0 to 15999
- old_embed: bfloat16 [16000, 5120], P('tensor', 'dp'), as said below
- expand_in: bfloat16 [8192, 5120], P('dp'), may hold values from -0.078125 to 0.078125
- query_out: bfloat16 [4096, 5120], P('tensor'), may hold values from -0.078125 to 0.078125
- key_out: bfloat16 [4096, 5120], P('tensor'), may hold values from -0.078125 to 0.078125
- old_query: bfloat16 [5120, 5120], P('dp', 'tensor'), may hold values from -0.078125 to 0.078125
- old_key: bfloat16 [5120, 5120], P('dp', 'tensor'), may hold values from -0.078125 to 0.078125
Outputs:
- grown_embedding: bfloat16 [16000, 8192], P('tensor', 'dp')
- grown_query: bfloat16 [8192, 4096], P('dp', 'tensor')
- grown_key: bfloat16 [8192, 4096], P('dp', 'tensor')
- attention_entropy: float32 [512, 32], P('dp', 'tensor')
The draws below stay inside these ranges and needn't reach their ends.
Inputs may be any that keep to these rules, and one draw needn't show every extreme that they name: `old_embed`: old embedding rows and features carry independent scales.
All inputs are finite; a program needn't handle non-finite values.
Results may differ from the reference program's by a relative error of at most 0.0097.
Values may be sent and summed in bfloat16 or wider, within the bound.
No kernel may reach another device: no remote copies, remote signals or barrier semaphores. Data moves between devices by JAX's collectives and lax.ppermute only.
A program may use at most 192 MiB of HBM per device.

```python
import math
import jax
import jax.numpy as jnp
from jax import lax

D_OLD = 5120
D_NEW = 8192
VOCAB = 16000
HEADS = 32
HEAD = 128
TOK_DP = 128
TOKENS = 512
N_DP = 4
N_TENSOR = 8


def draw_old_embed(key, part):
    first_key, second_key, third_key = jax.random.split(key, 3)
    row_scale = jnp.exp(jax.random.uniform(first_key, (VOCAB, 1), jnp.float32, math.log(0.3), math.log(3.0)))
    column_scale = jnp.exp(jax.random.uniform(second_key, (1, D_OLD), jnp.float32, math.log(0.4), math.log(4.0)))
    base_values = jax.random.normal(third_key, (VOCAB, D_OLD), jnp.float32)
    return (base_values * row_scale * column_scale).astype(jnp.bfloat16)


def plant(values, own_key, smallest, largest):
    longest = values.shape.index(max(values.shape))
    spots = []
    for shift in (0, 1):
        where = [jax.random.randint(jax.random.fold_in(own_key, axis), (), 0, length) for axis, length in enumerate(values.shape)]
        where[longest] = (where[longest] + shift) % values.shape[longest]
        spots.append(tuple(where))
    return values.at[spots[0]].set(smallest).at[spots[1]].set(largest)


def shard_levels(stream_key, extent, cuts, smallest, high):
    loudness, own = 1.0, jax.random.fold_in(stream_key, 6)
    for dim, shards_of in cuts:
        heights = jnp.exp(jax.random.uniform(jax.random.fold_in(own, dim), (shards_of,), jnp.float32, smallest / len(cuts), high / len(cuts)))
        loudness = loudness * jnp.repeat(heights, extent[dim] // shards_of).reshape([-1 if axis == dim else 1 for axis in range(len(extent))])
    return loudness


def centred(rng, shape, deviation, limit, pieces=(), held_as=jnp.bfloat16):
    loudness = shard_levels(rng, shape, pieces, -0.22, 0.18) if pieces else 1.0
    values = jax.random.normal(rng, shape, jnp.float32) * deviation * loudness
    return jnp.minimum(jnp.maximum(values, -limit), limit).astype(held_as)


def setup_inputs(seed: int = 0) -> dict:
    splits = jax.random.split(jax.random.key(seed), 8)
    return {
        "token_ids": plant(jax.random.randint(splits[0], (TOKENS,), 0, VOCAB), jax.random.fold_in(splits[0], 1), 0, VOCAB - 1).astype(jnp.int32),
        "old_embed": draw_old_embed(jax.random.fold_in(splits[7], 71), 0),
        "expand_in": centred(splits[2], (D_NEW, D_OLD), D_OLD ** -0.5, 0.078125, ((0, 4),)),
        "query_out": centred(splits[3], (HEADS * HEAD, D_OLD), D_OLD ** -0.5, 0.078125, ((0, 8),)),
        "key_out": centred(splits[4], (HEADS * HEAD, D_OLD), D_OLD ** -0.5, 0.078125, ((0, 8),)),
        "old_query": centred(splits[5], (D_OLD, D_OLD), D_OLD ** -0.5, 0.078125, ((0, 4), (1, 8))),
        "old_key": centred(splits[6], (D_OLD, D_OLD), D_OLD ** -0.5, 0.078125, ((0, 4), (1, 8))),
    }


EMBED_EPSILON = 1e-06
TOKEN_EPSILON = 1e-05

def grow_rows(row_block, expand_in):
    raw_rows = jnp.dot(row_block, expand_in.T, preferred_element_type=jnp.float32)
    old_ms = lax.optimization_barrier(jnp.mean(jnp.square(row_block.astype(jnp.float32)), axis=1))
    new_ms = lax.optimization_barrier(jnp.mean(jnp.square(raw_rows), axis=1))
    factor = jnp.sqrt((old_ms + EMBED_EPSILON) / (new_ms + EMBED_EPSILON))
    return (raw_rows * factor[:, None]).astype(jnp.bfloat16)

def rotate(values):
    half_size = HEAD // 2
    position = jnp.arange(TOK_DP).astype(jnp.float32)
    frequency = jnp.exp(-math.log(10000.0) * jnp.arange(half_size).astype(jnp.float32) * (2.0 / HEAD))
    angles = position[:, None] * frequency[None, :]
    cosine = jnp.cos(angles)[None, :, None, :]
    sine_table = jnp.sin(angles)[None, :, None, :]
    first_half = values[..., :half_size]
    second = values[..., half_size:]
    return jnp.concatenate([first_half * cosine - second * sine_table, second * cosine + first_half * sine_table], axis=-1)

def reference(token_ids, old_embed, expand_in, query_out, key_out, old_query, old_key):
    blocks = old_embed.reshape(N_TENSOR, VOCAB // N_TENSOR, D_OLD)
    grown_embedding = lax.map(lambda row_block: grow_rows(row_block, expand_in), blocks).reshape(VOCAB, D_NEW)
    inner_query = jnp.dot(query_out, old_query.T, preferred_element_type=jnp.float32).astype(jnp.bfloat16)
    inner_key = jnp.dot(key_out, old_key.T, preferred_element_type=jnp.float32).astype(jnp.bfloat16)
    grown_query = jnp.dot(expand_in, inner_query.T, preferred_element_type=jnp.float32).astype(jnp.bfloat16)
    grown_key = jnp.dot(expand_in, inner_key.T, preferred_element_type=jnp.float32).astype(jnp.bfloat16)
    hidden = jnp.take(grown_embedding, token_ids, axis=0)
    inverse_rms = lax.rsqrt(lax.optimization_barrier(jnp.mean(jnp.square(hidden.astype(jnp.float32)), axis=1)) + TOKEN_EPSILON)
    queries = jnp.dot(hidden, grown_query, preferred_element_type=jnp.float32) * inverse_rms[:, None]
    key_proj = jnp.dot(hidden, grown_key, preferred_element_type=jnp.float32) * inverse_rms[:, None]
    rotated_q = rotate(queries.reshape(N_DP, TOK_DP, HEADS, HEAD)).astype(jnp.bfloat16)
    rotated_k = rotate(key_proj.reshape(N_DP, TOK_DP, HEADS, HEAD)).astype(jnp.bfloat16)
    scores = jnp.einsum('sihd,sjhd->shij', rotated_q.astype(jnp.float32), rotated_k.astype(jnp.float32)) * HEAD ** (-0.5)
    causal = jnp.arange(TOK_DP)[:, None] >= jnp.arange(TOK_DP)[None, :]
    weights = jnp.where(causal[None, None], jnp.exp(scores), 0.0)
    weight_sum = lax.optimization_barrier(jnp.sum(weights, axis=-1))
    entropy = jnp.log(weight_sum) - lax.optimization_barrier(jnp.sum(weights * scores, axis=-1)) / weight_sum
    attention_entropy = jnp.transpose(entropy, (0, 2, 1)).reshape(TOKENS, HEADS)
    return (grown_embedding, grown_query, grown_key, attention_entropy)
```

```python
import functools
import math

import jax
import jax.numpy as jnp
from jax import lax
from jax.experimental import pallas as pl
from jax.experimental.pallas import tpu as pltpu
from jax.sharding import PartitionSpec as P

D_NEW = 8192
HEAD = 128


EMBED_EPSILON = 1e-06
TOKEN_EPSILON = 1e-05


def contract_last(left_side, right_side):
    return lax.dot_general(
        left_side, right_side, (((1,), (1,)), ((), ())), preferred_element_type=jnp.float32
    )


def rotate(values, head_count):
    row_count = values.shape[0]
    shaped = values.reshape(row_count, head_count, HEAD)
    half_size = HEAD // 2
    position = jnp.arange(row_count).astype(jnp.float32)
    frequency = jnp.exp(
        -math.log(10000.0) * jnp.arange(half_size).astype(jnp.float32) * (2.0 / HEAD)
    )
    angles = position[:, None] * frequency[None, :]
    cosine = jnp.cos(angles)[:, None, :]
    sine_table = jnp.sin(angles)[:, None, :]
    first_half = shaped[..., :half_size]
    second = shaped[..., half_size:]
    return jnp.concatenate(
        [first_half * cosine - second * sine_table, second * cosine + first_half * sine_table],
        axis=-1,
    )


def entropy_of(queries, key_proj, head_count):
    rotated_q = rotate(queries, head_count).astype(jnp.bfloat16)
    rotated_k = rotate(key_proj, head_count).astype(jnp.bfloat16)
    scores = jnp.einsum(
        "ihd,jhd->hij", rotated_q, rotated_k, preferred_element_type=jnp.float32
    ) * HEAD ** (-0.5)
    row_count = queries.shape[0]
    causal = jnp.arange(row_count)[:, None] >= jnp.arange(row_count)[None, :]
    weights = jnp.where(causal[None], jnp.exp(scores), 0.0)
    weight_sum = jnp.sum(weights, axis=-1)
    entropy = jnp.log(weight_sum) - jnp.sum(weights * scores, axis=-1) / weight_sum
    return entropy.T


def plain_plan(token_ids, old_embed, expand_in, query_out, key_out, old_query, old_key):
    vocab_rows = old_embed.shape[0]
    old_width = expand_in.shape[1]
    head_cols = query_out.shape[0]
    head_count = head_cols // HEAD
    shard_piece = lax.all_gather(old_embed, "dp", axis=1, tiled=True)
    operator_slab = expand_in
    raw_rows = contract_last(shard_piece, operator_slab)
    old_squares = jnp.sum(jnp.square(shard_piece.astype(jnp.float32)), axis=1)
    raw_rows, old_squares = (raw_rows, old_squares)
    new_squares = lax.psum(jnp.sum(jnp.square(raw_rows), axis=1), "dp")
    factor = jnp.sqrt(
        (old_squares / old_width + EMBED_EPSILON) / (new_squares / D_NEW + EMBED_EPSILON)
    )
    grown_embedding = (raw_rows * factor[:, None]).astype(jnp.bfloat16)
    pieces = (
        lax.all_gather(old_query, "tensor", axis=1, tiled=True),
        lax.all_gather(old_key, "tensor", axis=1, tiled=True),
    )
    inner_query = contract_last(query_out, pieces[0])
    inner_key = contract_last(key_out, pieces[1])
    inner_query = inner_query.astype(jnp.bfloat16)
    inner_key = inner_key.astype(jnp.bfloat16)
    pieces = (
        lax.all_gather(inner_query, "dp", axis=1, tiled=True),
        lax.all_gather(inner_key, "dp", axis=1, tiled=True),
    )
    operator_slab = expand_in
    grown_q32 = contract_last(operator_slab, pieces[0])
    grown_k32 = contract_last(operator_slab, pieces[1])
    grown_query = grown_q32.astype(jnp.bfloat16)
    grown_key = grown_k32.astype(jnp.bfloat16)
    offset_ids = token_ids - lax.axis_index("tensor") * vocab_rows
    inside = (offset_ids >= 0) & (offset_ids < vocab_rows)
    picked = jnp.take(grown_embedding, jnp.clip(offset_ids, 0, vocab_rows - 1), axis=0)
    partial_rows = jnp.where(inside[:, None], picked.astype(jnp.float32), 0.0)
    hidden_cols = lax.psum(partial_rows.astype(jnp.bfloat16), "tensor")
    partial_term = jnp.concatenate(
        [
            jnp.dot(hidden_cols, grown_query, preferred_element_type=jnp.float32),
            jnp.dot(hidden_cols, grown_key, preferred_element_type=jnp.float32),
        ],
        axis=1,
    )
    squares = jnp.sum(jnp.square(hidden_cols.astype(jnp.float32)), axis=1)
    summed_tokens, square_sum = (
        lax.psum_scatter(partial_term, "dp", scatter_dimension=0, tiled=True),
        lax.psum_scatter(squares, "dp", scatter_dimension=0, tiled=True),
    )
    queries = summed_tokens[:, :head_cols]
    key_proj = summed_tokens[:, head_cols:]
    inverse_rms = lax.rsqrt(square_sum / D_NEW + TOKEN_EPSILON)
    queries = queries * inverse_rms[:, None]
    key_proj = key_proj * inverse_rms[:, None]
    attention_entropy = entropy_of(queries, key_proj, head_count)
    return (grown_embedding, grown_query, grown_key, attention_entropy)


VMEM_BYTES = 48 * 1024 * 1024
SMALL_COST = pl.CostEstimate(flops=1024, bytes_accessed=1024, transcendentals=0)
EMBED_ROWS = (512, 512, 448, 528)


def permute_dp(values, flip):
    return lax.ppermute(values, "dp", [(source, source ^ flip) for source in range(4)])


def permute_tensor(values, pairs):
    return lax.ppermute(
        values, "tensor", [(a * 2 + core, b * 2 + core) for a, b in pairs for core in range(2)]
    )


def swap_core(values):
    return lax.ppermute(values, "tensor", [(a, a ^ 1) for a in range(8)])


SWAP_NEAR = [(0, 1), (1, 0), (2, 3), (3, 2)]
SWAP_FAR = [(0, 2), (2, 0), (1, 3), (3, 1)]


def sum_dp(values):
    values = values + permute_dp(values, 1)
    return values + permute_dp(values, 2)


def keep_half(values, bit, exchange):
    half = values.shape[0] // 2
    mine = lax.dynamic_slice_in_dim(values, bit * half, half)
    theirs = lax.dynamic_slice_in_dim(values, (1 - bit) * half, half)
    return mine + exchange(theirs)


def join_half(values, bit, exchange):
    theirs = exchange(values)
    first = jnp.where(bit == 0, values, theirs)
    second = jnp.where(bit == 0, theirs, values)
    return jnp.concatenate([first, second], axis=0)


def split_rows(row_count):
    return -(-row_count // 32) * 16


def slabs_of(expand_in, tile):
    block = expand_in.shape[1] // 4
    return [pl.BlockSpec((tile, block), lambda n, order, k=k: (n, order[k])) for k in range(4)]


def embed_kernel(order, own, from_x, from_y, top, bottom, e0, e1, e2, e3, raw, squares):
    far = jnp.concatenate([contract_last(top[...], e3[...]), contract_last(bottom[...], e3[...])], axis=0)
    total = (
        contract_last(own[...], e0[...])
        + contract_last(from_x[...], e1[...])
        + contract_last(from_y[...], e2[...])
        + far
    )
    raw[...] = total

    @pl.when(pl.program_id(0) == 0)
    def _():
        squares[...] = jnp.zeros_like(squares)

    squared = total * total
    lanes = squared[:, :HEAD]
    for column in range(HEAD, squared.shape[1], HEAD):
        lanes = lanes + squared[:, column : column + HEAD]
    squares[...] += lanes


def embed_rows(order, copies, expand_in, tile=512):
    row_count = copies[0].shape[0]
    new_width, old_width = expand_in.shape
    whole = lambda a: pl.BlockSpec(a.shape, lambda n, order: (0, 0))
    return pl.pallas_call(
        embed_kernel,
        grid_spec=pltpu.PrefetchScalarGridSpec(
            num_scalar_prefetch=1,
            grid=(new_width // tile,),
            in_specs=[whole(a) for a in copies] + slabs_of(expand_in, tile),
            out_specs=[
                pl.BlockSpec((row_count, tile), lambda n, order: (0, n)),
                pl.BlockSpec((row_count, HEAD), lambda n, order: (0, 0)),
            ],
        ),
        out_shape=[
            jax.ShapeDtypeStruct((row_count, new_width), jnp.float32),
            jax.ShapeDtypeStruct((row_count, HEAD), jnp.float32),
        ],
        compiler_params=pltpu.CompilerParams(vmem_limit_bytes=VMEM_BYTES),
        cost_estimate=SMALL_COST,
        name="embed_rows",
    )(order, *copies, *([expand_in] * 4))


def grown_kernel(terms, has_base, order, *refs):
    grown = refs[-1]
    slabs = refs[-5:-1]
    total = refs[-6][...] if has_base else 0.0
    rest = iter(refs)
    for copy, offset, width, parts in terms:
        ref = [next(rest) for _ in range(parts)]
        found = [contract_last(slabs[copy][:, pl.ds(offset, width)], part[...]) for part in ref]
        total += found[0] if len(found) == 1 else jnp.concatenate(found, axis=1)
    grown[...] = total.astype(grown.dtype)


def grow_projection(order, terms, expand_in, base=None, dtype=jnp.bfloat16, tile=512):
    new_width = expand_in.shape[0]
    arrays = [array for _, _, parts in terms for array in parts]
    columns = sum(array.shape[0] for array in terms[0][2])
    places = tuple((copy, offset, parts[0].shape[1], len(parts)) for copy, offset, parts in terms)
    whole = lambda a: pl.BlockSpec(a.shape, lambda n, order: (0, 0))
    tiles = pl.BlockSpec((tile, columns), lambda n, order: (n, 0))
    return pl.pallas_call(
        functools.partial(grown_kernel, places, base is not None),
        grid_spec=pltpu.PrefetchScalarGridSpec(
            num_scalar_prefetch=1,
            grid=(new_width // tile,),
            in_specs=[whole(a) for a in arrays] + [tiles] * (base is not None) + slabs_of(expand_in, tile),
            out_specs=tiles,
        ),
        out_shape=jax.ShapeDtypeStruct((new_width, columns), dtype),
        compiler_params=pltpu.CompilerParams(vmem_limit_bytes=VMEM_BYTES),
        cost_estimate=SMALL_COST,
        name="grow_projection",
    )(order, *arrays, *([base] * (base is not None)), *([expand_in] * 4))


def row_factor(old_squares, old_width, new_squares):
    return jnp.sqrt(
        (old_squares / old_width + EMBED_EPSILON) / (new_squares / D_NEW + EMBED_EPSILON)
    )


def scatter_tokens(partial):
    me = lax.axis_index("dp")
    partial = keep_half(partial, me // 2, lambda v: permute_dp(v, 2))
    return keep_half(partial, me % 2, lambda v: permute_dp(v, 1))


KEY_SPLIT = 1024


def ring_plan(token_ids, old_embed, expand_in, query_out, key_out, old_query, old_key):
    vocab_rows = old_embed.shape[0]
    new_width, old_width = expand_in.shape
    head_cols = query_out.shape[0]
    head_count = head_cols // HEAD
    me = lax.axis_index("dp")
    order = jnp.stack([me, me ^ 1, me ^ 2, me ^ 3]).astype(jnp.int32)
    here = lax.axis_index("tensor")
    chip, core = here // 2, here % 2
    block = old_query.shape[0]
    got = {}

    def after(values, *keys):
        values, found = lax.optimization_barrier((values, [got[key] for key in keys]))
        got.update(zip(keys, found))
        return values

    got["old", "q"] = lax.all_gather(old_query, "tensor", axis=1, tiled=True)
    got["old", "k0"] = lax.all_gather(old_key[:KEY_SPLIT], "tensor", axis=1, tiled=True)
    got["old", "k1"] = lax.all_gather(old_key[KEY_SPLIT:], "tensor", axis=1, tiled=True)

    def inner(name, *keys):
        out_operator = query_out if name == "q" else key_out
        found = contract_last(out_operator, after(got["old", name], *keys))
        got["own", name] = found.astype(jnp.bfloat16)

    def spread_near(name):
        with jax.named_scope(f"near_{name}"):
            got["x", name], got["y", name] = permute_dp(got["own", name], 1), permute_dp(got["own", name], 2)

    def spread_far(name):
        cut = split_rows(got["x", name].shape[0])
        with jax.named_scope(f"far_{name}"):
            got["top", name] = permute_dp(got["x", name][:cut], 2)
            got["bottom", name] = permute_dp(got["y", name][cut:], 1)

    def ready(keys, *before):
        found = after([got[key] for key in keys], *before)
        got.update(zip(keys, found))

    def copies(name):
        return [got[kind, name] for kind in ("own", "x", "y", "top", "bottom")]

    starts = [sum(EMBED_ROWS[:n]) for n in range(len(EMBED_ROWS) + 1)]
    for n in range(len(EMBED_ROWS)):
        got["own", n] = old_embed[starts[n] : starts[n + 1]]
    embedding = [jnp.zeros((vocab_rows, new_width), jnp.bfloat16)]
    old_own = jnp.sum(jnp.square(old_embed.astype(jnp.float32)), axis=1)

    def embed(n, *keys):
        arrays = copies(n)
        arrays[0] = after(arrays[0], *keys)
        got["raw", n], got["squares", n] = embed_rows(order, arrays, expand_in)

    def sum_rows(first, last, *keys):
        count = lambda n: starts[n + 1] - starts[n]
        mine = [jnp.sum(got["squares", n][: count(n)], axis=1) for n in range(first, last)]
        mine = jnp.stack([old_own[starts[first] : starts[last]], jnp.concatenate(mine)])
        with jax.named_scope(f"sums_{first}"):
            got["sums", first] = sum_dp(after(mine, *keys))

    def rescale(first, last, *keys):
        sums = after(got["sums", first], *keys)
        factors = row_factor(sums[0], old_width, sums[1])
        for n in range(first, last):
            factor = factors[starts[n] - starts[first] : starts[n + 1] - starts[first]]
            raw = got["raw", n][: factor.shape[0]]
            embedding[0] = lax.dynamic_update_slice(
                embedding[0], (raw * factor[:, None]).astype(jnp.bfloat16), (starts[n], 0)
            )

    def token_term(name, first, last):
        return contract_last(got["shrunk"][:, first:last], got["own", name])

    near_z = lambda v: permute_tensor(v, SWAP_NEAR)
    far_z = lambda v: permute_tensor(v, SWAP_FAR)

    def tokens_share():
        offset_ids = token_ids - here * vocab_rows
        inside = (offset_ids >= 0) & (offset_ids < vocab_rows)
        picked = jnp.take(old_embed, jnp.clip(offset_ids, 0, vocab_rows - 1), axis=0)
        picked = jnp.where(inside[:, None], picked, jnp.zeros_like(picked))
        with jax.named_scope("token_share"):
            share = keep_half(picked, core, swap_core)
            share = keep_half(share, chip % 2, near_z)
            got["share"] = after(share, ("x", 0), ("y", 0))
            got["share"] = keep_half(got["share"], chip // 2, far_z)

    def tokens_shrink():
        last = starts[3] - starts[2]
        share, raw = got["own", 2][last:], got["raw", 2][last:]
        rounded = raw.astype(jnp.bfloat16)
        partial = jnp.dot(rounded, expand_in, preferred_element_type=jnp.float32)
        squares = [jnp.sum(jnp.square(v.astype(jnp.float32)), axis=1) for v in (share, raw, rounded)]
        squares = [jnp.broadcast_to(v[:, None], (v.shape[0], HEAD)) for v in squares]
        cuts = [partial[:, n * block : (n + 1) * block] for n in range(4)]
        got["parts"] = jnp.stack([jnp.concatenate([cut, *squares], axis=1) for cut in cuts])

    def tokens_sum(*keys):
        with jax.named_scope("token_sum"):
            parts = keep_half(got["parts"], me // 2, lambda v: permute_dp(v, 2))
            parts = after(parts, *keys)
            got["shrink"] = keep_half(parts, me % 2, lambda v: permute_dp(v, 1))[0]

    def tokens_all():
        total = got["shrink"]
        old_sums, new_sums, hidden_sums = (total[:, block + n * HEAD] for n in range(3))
        factor = row_factor(old_sums, old_width, new_sums)
        inverse_rms = lax.rsqrt(hidden_sums * jnp.square(factor) / D_NEW + TOKEN_EPSILON)
        shrunk = (total[:, :block] * (factor * inverse_rms)[:, None]).astype(jnp.bfloat16)
        with jax.named_scope("token_all"):
            share = join_half(after(shrunk, ("own", "k0")), chip // 2, far_z)
            share = join_half(after(share, ("own", "k1")), chip % 2, near_z)
            got["shrunk"] = join_half(share, core, swap_core)

    def term(name, kind, offset=0):
        number = ("own", "x", "y", "far").index(kind)
        parts = [got[kind, name]] if kind != "far" else [got["top", name], got["bottom", name]]
        return number, offset, parts

    every = ("own", "x", "y", "far")
    arrived = lambda near=None, far=None: (
        *((("x", near), ("y", near)) if near is not None else ()),
        *((("top", far), ("bottom", far)) if far is not None else ()),
    )
    spread_near(0)
    tokens_share()
    ready([("own", 1), ("x", 0), ("y", 0)])
    ready([("own", 1)], *arrived(0))
    spread_near(1)
    spread_far(0)
    got["own", 2] = jnp.concatenate([got["own", 2], got["share"]], axis=0)
    ready([("own", 2), *arrived(1)], *arrived(far=0))
    spread_near(2)
    spread_far(1)
    embed(0, *arrived(1))
    ready([("own", 3), *arrived(2)], ("squares", 0), *arrived(far=1))
    spread_near(3)
    spread_far(2)
    embed(1)
    inner("q", ("squares", 1))
    ready([("own", "q"), *arrived(3)], *arrived(far=2))
    spread_near("q")
    spread_far(3)
    embed(2, *arrived(3), ("own", "q"))
    tokens_shrink()
    ready(["parts", *arrived("q")], *arrived(far=3))
    tokens_sum(*arrived("q"))
    spread_far("q")
    embed(3, "parts")
    sum_rows(0, 4, *arrived(far="q"))
    inner("k0", ("squares", 3))
    ready([("own", "k0")], *arrived(far="q"))
    spread_near("k0")
    rescale(0, 4, ("own", "k0"))
    ready([("own", "q")], ("own", "k0"))
    got["grown", "q"] = grow_projection(order, [term("q", kind) for kind in every], expand_in)
    ready([*arrived("k0")], ("grown", "q"))
    spread_far("k0")
    inner("k1", ("grown", "q"))
    with jax.named_scope("near_k1"):
        for kind, flip in (("x", 1), ("y", 2), ("top", 3)):
            got[kind, "k1"] = permute_dp(got["own", "k1"], flip)
    tokens_all()
    got["tokens", "q"] = scatter_tokens(token_term("q", 0, block))
    got["tokens", "k"] = scatter_tokens(
        token_term("k0", 0, KEY_SPLIT) + token_term("k1", KEY_SPLIT, block)
    )
    ready([("own", "k0")], ("own", "k1"))
    grown_key = grow_projection(
        order, [term("k0", kind) for kind in every[:3]], expand_in, dtype=jnp.float32
    )
    last_terms = [term("k1", kind, KEY_SPLIT) for kind in every[:3]]
    last_terms += [(3, KEY_SPLIT, [got["top", "k1"]]), term("k0", "far")]
    grown_key = grow_projection(order, last_terms, expand_in, grown_key)
    attention_entropy = entropy_of(got["tokens", "q"], got["tokens", "k"], head_count)
    return embedding[0], got["grown", "q"], grown_key, attention_entropy


def solution(mesh):
    placed = (
        P(),
        P("tensor", "dp"),
        P("dp", None),
        P("tensor", None),
        P("tensor", None),
        P("dp", "tensor"),
        P("dp", "tensor"),
    )
    return jax.shard_map(
        ring_plan if (mesh.shape["dp"], mesh.shape["tensor"]) == (4, 8) else plain_plan,
        mesh=mesh,
        in_specs=placed,
        out_specs=(P("tensor", "dp"), P("dp", "tensor"), P("dp", "tensor"), P("dp", "tensor")),
        check_vma=False,
    )
```

```python
import functools
import math

import jax
import jax.numpy as jnp
from jax import lax
from jax.experimental import pallas as pl
from jax.experimental.pallas import tpu as pltpu
from jax.sharding import PartitionSpec as P

D_NEW = 8192
HEAD = 128


EMBED_EPSILON = 1e-06
TOKEN_EPSILON = 1e-05


def contract_last(left_side, right_side):
    return lax.dot_general(
        left_side, right_side, (((1,), (1,)), ((), ())), preferred_element_type=jnp.float32
    )


def rotate(values, head_count):
    row_count = values.shape[0]
    shaped = values.reshape(row_count, head_count, HEAD)
    half_size = HEAD // 2
    position = jnp.arange(row_count).astype(jnp.float32)
    frequency = jnp.exp(
        -math.log(10000.0) * jnp.arange(half_size).astype(jnp.float32) * (2.0 / HEAD)
    )
    angles = position[:, None] * frequency[None, :]
    cosine = jnp.cos(angles)[:, None, :]
    sine_table = jnp.sin(angles)[:, None, :]
    first_half = shaped[..., :half_size]
    second = shaped[..., half_size:]
    return jnp.concatenate(
        [first_half * cosine - second * sine_table, second * cosine + first_half * sine_table],
        axis=-1,
    )


def entropy_of(queries, key_proj, head_count):
    rotated_q = rotate(queries, head_count).astype(jnp.bfloat16)
    rotated_k = rotate(key_proj, head_count).astype(jnp.bfloat16)
    scores = jnp.einsum(
        "ihd,jhd->hij", rotated_q, rotated_k, preferred_element_type=jnp.float32
    ) * HEAD ** (-0.5)
    row_count = queries.shape[0]
    causal = jnp.arange(row_count)[:, None] >= jnp.arange(row_count)[None, :]
    weights = jnp.where(causal[None], jnp.exp(scores), 0.0)
    weight_sum = jnp.sum(weights, axis=-1)
    entropy = jnp.log(weight_sum) - jnp.sum(weights * scores, axis=-1) / weight_sum
    return entropy.T


def plain_plan(token_ids, old_embed, expand_in, query_out, key_out, old_query, old_key):
    vocab_rows = old_embed.shape[0]
    old_width = expand_in.shape[1]
    head_cols = query_out.shape[0]
    head_count = head_cols // HEAD
    shard_piece = lax.all_gather(old_embed, "dp", axis=1, tiled=True)
    operator_slab = expand_in
    raw_rows = contract_last(shard_piece, operator_slab)
    old_squares = jnp.sum(jnp.square(shard_piece.astype(jnp.float32)), axis=1)
    raw_rows, old_squares = (raw_rows, old_squares)
    new_squares = lax.psum(jnp.sum(jnp.square(raw_rows), axis=1), "dp")
    factor = jnp.sqrt(
        (old_squares / old_width + EMBED_EPSILON) / (new_squares / D_NEW + EMBED_EPSILON)
    )
    grown_embedding = (raw_rows * factor[:, None]).astype(jnp.bfloat16)
    pieces = (
        lax.all_gather(old_query, "tensor", axis=1, tiled=True),
        lax.all_gather(old_key, "tensor", axis=1, tiled=True),
    )
    inner_query = contract_last(query_out, pieces[0])
    inner_key = contract_last(key_out, pieces[1])
    inner_query = inner_query.astype(jnp.bfloat16)
    inner_key = inner_key.astype(jnp.bfloat16)
    pieces = (
        lax.all_gather(inner_query, "dp", axis=1, tiled=True),
        lax.all_gather(inner_key, "dp", axis=1, tiled=True),
    )
    operator_slab = expand_in
    grown_q32 = contract_last(operator_slab, pieces[0])
    grown_k32 = contract_last(operator_slab, pieces[1])
    grown_query = grown_q32.astype(jnp.bfloat16)
    grown_key = grown_k32.astype(jnp.bfloat16)
    offset_ids = token_ids - lax.axis_index("tensor") * vocab_rows
    inside = (offset_ids >= 0) & (offset_ids < vocab_rows)
    picked = jnp.take(grown_embedding, jnp.clip(offset_ids, 0, vocab_rows - 1), axis=0)
    partial_rows = jnp.where(inside[:, None], picked.astype(jnp.float32), 0.0)
    hidden_cols = lax.psum(partial_rows.astype(jnp.bfloat16), "tensor")
    partial_term = jnp.concatenate(
        [
            jnp.dot(hidden_cols, grown_query, preferred_element_type=jnp.float32),
            jnp.dot(hidden_cols, grown_key, preferred_element_type=jnp.float32),
        ],
        axis=1,
    )
    squares = jnp.sum(jnp.square(hidden_cols.astype(jnp.float32)), axis=1)
    summed_tokens, square_sum = (
        lax.psum_scatter(partial_term, "dp", scatter_dimension=0, tiled=True),
        lax.psum_scatter(squares, "dp", scatter_dimension=0, tiled=True),
    )
    queries = summed_tokens[:, :head_cols]
    key_proj = summed_tokens[:, head_cols:]
    inverse_rms = lax.rsqrt(square_sum / D_NEW + TOKEN_EPSILON)
    queries = queries * inverse_rms[:, None]
    key_proj = key_proj * inverse_rms[:, None]
    attention_entropy = entropy_of(queries, key_proj, head_count)
    return (grown_embedding, grown_query, grown_key, attention_entropy)


VMEM_BYTES = 48 * 1024 * 1024
SMALL_COST = pl.CostEstimate(flops=1024, bytes_accessed=1024, transcendentals=0)
EMBED_ROWS = (464, 560, 656, 320)


def permute_dp(values, flip):
    return lax.ppermute(values, "dp", [(source, source ^ flip) for source in range(4)])


def permute_tensor(values, pairs):
    return lax.ppermute(
        values, "tensor", [(a * 2 + core, b * 2 + core) for a, b in pairs for core in range(2)]
    )


def swap_core(values):
    return lax.ppermute(values, "tensor", [(a, a ^ 1) for a in range(8)])


def permute_chip(values, flip):
    return permute_tensor(values, [(chip, chip ^ flip) for chip in range(4)])


def sum_dp(values):
    values = values + permute_dp(values, 1)
    return values + permute_dp(values, 2)


def keep_half(values, bit, exchange):
    half = values.shape[0] // 2
    mine = lax.dynamic_slice_in_dim(values, bit * half, half)
    theirs = lax.dynamic_slice_in_dim(values, (1 - bit) * half, half)
    return mine + exchange(theirs)


def join_half(values, bit, exchange):
    theirs = exchange(values)
    first = jnp.where(bit == 0, values, theirs)
    second = jnp.where(bit == 0, theirs, values)
    return jnp.concatenate([first, second], axis=0)


def split_rows(row_count):
    return -(-row_count // 32) * 16


def slabs_of(expand_in, tile, first=0, width=None):
    block = expand_in.shape[1] // 4
    width = width or block
    at = lambda k: pl.BlockSpec(
        (tile, width), lambda n, order: (n, order[k] * (block // width) + first // width)
    )
    return [at(k) for k in range(4)]


def lane_sums(squared):
    lanes = squared[:, :HEAD]
    for column in range(HEAD, squared.shape[1], HEAD):
        lanes = lanes + squared[:, column : column + HEAD]
    return lanes


def embed_kernel(places, tokens, order, *refs):
    arrays = [ref[first : first + count] for ref, (first, count) in zip(refs, places)]
    own, from_x, from_y, top, bottom = arrays
    e0, e1, e2, e3, raw, squares, *shrunk = refs[5:]
    far = jnp.concatenate([contract_last(top, e3[...]), contract_last(bottom, e3[...])], axis=0)
    total = (
        contract_last(own, e0[...])
        + contract_last(from_x, e1[...])
        + contract_last(from_y, e2[...])
        + far
    )
    raw[...] = total
    first = total.shape[0] - tokens
    width = own.shape[1]

    @pl.when(pl.program_id(0) == 0)
    def _():
        squares[:, :HEAD] = lane_sums(jnp.square(own.astype(jnp.float32)))
        squares[:, HEAD:] = jnp.zeros_like(squares[:, HEAD:])
        if tokens:
            for copy in range(4):
                part = shrunk[copy // 2]
                part[copy % 2] = jnp.zeros_like(part[copy % 2])
                part[copy % 2, :, width : width + HEAD] = squares[first:, :HEAD]

    squares[:, HEAD:] += lane_sums(total * total)
    if tokens:
        found = total[first:]
        rounded = found.astype(jnp.bfloat16)
        again = rounded.astype(jnp.float32)
        sums = jnp.concatenate([lane_sums(found * found), lane_sums(again * again)], axis=1)
        for copy, slab in enumerate((e0, e1, e2, e3)):
            part = shrunk[copy // 2]
            part[copy % 2, :, :width] += jnp.dot(rounded, slab[...], preferred_element_type=jnp.float32)
            part[copy % 2, :, width + HEAD :] += sums


def embed_rows(order, copies, expand_in, tokens=0, tile=512):
    arrays = [array for array, _, _ in copies]
    places = tuple((first, count) for _, first, count in copies)
    row_count, block = arrays[0].shape
    new_width = expand_in.shape[0]
    whole = lambda a: pl.BlockSpec(a.shape, lambda n, order: (0, 0))
    out_specs = [
        pl.BlockSpec((row_count, tile), lambda n, order: (0, n)),
        pl.BlockSpec((row_count, 2 * HEAD), lambda n, order: (0, 0)),
    ]
    out_shape = [
        jax.ShapeDtypeStruct((row_count, new_width), jnp.float32),
        jax.ShapeDtypeStruct((row_count, 2 * HEAD), jnp.float32),
    ]
    if tokens:
        shrunk = (2, tokens, block + 3 * HEAD)
        out_specs += [pl.BlockSpec(shrunk, lambda n, order: (0, 0, 0))] * 2
        out_shape += [jax.ShapeDtypeStruct(shrunk, jnp.float32)] * 2
    return pl.pallas_call(
        functools.partial(embed_kernel, places, tokens),
        grid_spec=pltpu.PrefetchScalarGridSpec(
            num_scalar_prefetch=1,
            grid=(new_width // tile,),
            in_specs=[whole(a) for a in arrays] + slabs_of(expand_in, tile),
            out_specs=out_specs,
        ),
        out_shape=out_shape,
        compiler_params=pltpu.CompilerParams(vmem_limit_bytes=VMEM_BYTES),
        cost_estimate=pl.CostEstimate(
            flops=2 * row_count * 4 * block * new_width, bytes_accessed=8 * block * new_width, transcendentals=0
        ),
        name="embed_rows",
    )(order, *arrays, *([expand_in] * 4))


def grown_kernel(terms, has_base, order, *refs):
    grown = refs[-1]
    slabs = refs[-5:-1]
    total = refs[-6][...] if has_base else 0.0
    rest = iter(refs)
    for copy, offset, width, parts in terms:
        found = [
            contract_last(slabs[copy][:, pl.ds(offset, width)], next(rest)[first : first + count])
            for first, count in parts
        ]
        total += found[0] if len(found) == 1 else jnp.concatenate(found, axis=1)
    grown[...] = total.astype(grown.dtype)


def grow_projection(order, terms, expand_in, base=None, dtype=jnp.bfloat16, first=0, width=None, tile=512):
    new_width = expand_in.shape[0]
    arrays = [array for _, _, parts in terms for array, _, _ in parts]
    columns = sum(count for _, _, count in terms[0][2])
    places = tuple(
        (copy, offset, parts[0][0].shape[1], tuple(part[1:] for part in parts))
        for copy, offset, parts in terms
    )
    whole = lambda a: pl.BlockSpec(a.shape, lambda n, order: (0, 0))
    tiles = pl.BlockSpec((tile, columns), lambda n, order: (n, 0))
    return pl.pallas_call(
        functools.partial(grown_kernel, places, base is not None),
        grid_spec=pltpu.PrefetchScalarGridSpec(
            num_scalar_prefetch=1,
            grid=(new_width // tile,),
            in_specs=[whole(a) for a in arrays] + [tiles] * (base is not None) + slabs_of(expand_in, tile, first, width),
            out_specs=tiles,
        ),
        out_shape=jax.ShapeDtypeStruct((new_width, columns), dtype),
        compiler_params=pltpu.CompilerParams(vmem_limit_bytes=VMEM_BYTES),
        cost_estimate=pl.CostEstimate(
            flops=2 * new_width * sum(array.size for array in arrays),
            bytes_accessed=2 * expand_in.size,
            transcendentals=0,
        ),
        name="grow_projection",
    )(order, *arrays, *([base] * (base is not None)), *([expand_in] * 4))


def inner_kernel(operator, old, found):
    found[...] = contract_last(operator[...], old[...]).astype(found.dtype)


def inner_product(operator, old, tile=256):
    rows, depth = operator.shape
    columns = old.shape[0]
    return pl.pallas_call(
        inner_kernel,
        grid=(columns // tile,),
        in_specs=[
            pl.BlockSpec((rows, depth), lambda n: (0, 0)),
            pl.BlockSpec((tile, depth), lambda n: (n, 0)),
        ],
        out_specs=pl.BlockSpec((rows, tile), lambda n: (0, n)),
        out_shape=jax.ShapeDtypeStruct((rows, columns), jnp.bfloat16),
        compiler_params=pltpu.CompilerParams(vmem_limit_bytes=VMEM_BYTES),
        cost_estimate=SMALL_COST,
        name="inner_product",
    )(operator, old)


def row_factor(old_squares, old_width, new_squares):
    return jnp.sqrt(
        (old_squares / old_width + EMBED_EPSILON) / (new_squares / D_NEW + EMBED_EPSILON)
    )


def scatter_tokens(partial):
    share = partial.shape[0] // 4
    me = lax.axis_index("dp")
    cut = lambda flip: lax.dynamic_slice_in_dim(partial, (me ^ flip) * share, share)
    theirs = [permute_dp(cut(flip).astype(jnp.bfloat16), flip) for flip in (1, 2, 3)]
    return cut(0) + sum(part.astype(jnp.float32) for part in theirs)


KEY_SPLIT = 1024


def ring_plan(token_ids, old_embed, expand_in, query_out, key_out, old_query, old_key):
    vocab_rows = old_embed.shape[0]
    new_width, old_width = expand_in.shape
    head_cols = query_out.shape[0]
    head_count = head_cols // HEAD
    me = lax.axis_index("dp")
    order = jnp.stack([me, me ^ 1, me ^ 2, me ^ 3]).astype(jnp.int32)
    here = lax.axis_index("tensor")
    chip, core = here // 2, here % 2
    block = old_query.shape[0]
    got = {}

    def after(values, *keys):
        values, found = lax.optimization_barrier((values, [got[key] for key in keys]))
        got.update(zip(keys, found))
        return values

    got["old", "q"] = lax.all_gather(old_query, "tensor", axis=1, tiled=True)
    got["old", "k0"] = lax.all_gather(old_key[:KEY_SPLIT], "tensor", axis=1, tiled=True)
    got["old", "k1"] = lax.all_gather(old_key[KEY_SPLIT:], "tensor", axis=1, tiled=True)

    def inner(name, *keys):
        out_operator = query_out if name == "q" else key_out
        got["own", name] = inner_product(out_operator, after(got["old", name], *keys))

    def shift(name, previous=None):
        own = [] if name is None else [got["own", name]]
        to_x, to_y = list(own), list(own)
        if previous is not None:
            count = got["own", previous].shape[0]
            cut = split_rows(count)
            to_x.append(got["y", previous][cut:count])
            to_y.append(got["x", previous][:cut])
        key = name if name is not None else ("far", previous)
        with jax.named_scope(f"shift_{name}_{previous}"):
            got["x", key] = permute_dp(jnp.concatenate(to_x, axis=0), 1)
            got["y", key] = permute_dp(jnp.concatenate(to_y, axis=0), 2)

    def ready(keys, *before):
        found = after([got[key] for key in keys], *before)
        got.update(zip(keys, found))

    def arrived(*keys):
        return [(side, key) for key in keys for side in ("x", "y")]

    def copies(name, following):
        count = got["own", name].shape[0]
        cut = split_rows(count)
        base = got["own", following].shape[0] if ("own", following) in got else 0
        return [
            (got["own", name], 0, count),
            (got["x", name], 0, count),
            (got["y", name], 0, count),
            (got["y", following], base, cut),
            (got["x", following], base, count - cut),
        ]

    starts = [sum(EMBED_ROWS[:n]) for n in range(len(EMBED_ROWS) + 1)]
    for n in range(len(EMBED_ROWS)):
        got["own", n] = old_embed[starts[n] : starts[n + 1]]
    embedding = [jnp.zeros((vocab_rows, new_width), jnp.bfloat16)]

    def embed(n, following, *keys, tokens=0):
        ready([("own", n)], *keys)
        found = embed_rows(order, copies(n, following), expand_in, tokens)
        got["raw", n], got["squares", n], *parts = found
        if tokens:
            got["parts"] = parts

    def sum_rows(*keys):
        found = []
        for n in range(len(EMBED_ROWS)):
            lanes = got["squares", n][: starts[n + 1] - starts[n]]
            found.append([jnp.sum(lanes[:, :HEAD], axis=1), jnp.sum(lanes[:, HEAD:], axis=1)])
        found = jnp.stack([jnp.concatenate([pair[side] for pair in found]) for side in range(2)])
        with jax.named_scope("sums"):
            got["sums"] = sum_dp(after(found, *keys))

    def rescale(*keys):
        sums = after(got["sums"], *keys)
        factors = row_factor(sums[0], old_width, sums[1])
        for n in range(len(EMBED_ROWS)):
            factor = factors[starts[n] : starts[n + 1]]
            raw = got["raw", n][: factor.shape[0]]
            embedding[0] = lax.dynamic_update_slice(
                embedding[0], (raw * factor[:, None]).astype(jnp.bfloat16), (starts[n], 0)
            )

    def token_term(name, first, last):
        return contract_last(got["shrunk"][:, first:last], got["own", name])

    def tokens_share():
        offset_ids = token_ids - here * vocab_rows
        inside = (offset_ids >= 0) & (offset_ids < vocab_rows)
        picked = jnp.take(old_embed, jnp.clip(offset_ids, 0, vocab_rows - 1), axis=0)
        picked = jnp.where(inside[:, None], picked, jnp.zeros_like(picked))
        picked = picked.reshape(4, 2, -1, block)
        with jax.named_scope("token_share"):
            cut = lambda bit: lax.dynamic_index_in_dim(picked, bit, 1, keepdims=False)
            share = cut(core) + swap_core(cut(1 - core))
            share = share.reshape(2, 2, *share.shape[1:])
            half = lambda bit: lax.dynamic_index_in_dim(share, bit, 1, keepdims=False)
            got["half"] = half(chip % 2), permute_chip(half(1 - chip % 2), 1)

    def tokens_share_rest(*keys):
        mine, theirs = after(got["half"], *keys)
        with jax.named_scope("token_share"):
            got["share"] = keep_half(mine + theirs, chip // 2, lambda v: permute_chip(v, 2))[0]

    def tokens_y():
        near, far = got["parts"]
        with jax.named_scope("token_sum"):
            got["parts"] = near, permute_dp(far, 2)

    def tokens_x(*keys):
        mine, theirs = after(got["parts"], *keys)
        with jax.named_scope("token_sum"):
            parts = mine + theirs
            got["shrink"] = parts[0] + permute_dp(parts[1], 1)

    def tokens_all(*keys):
        total = after(got["shrink"], *keys)
        sums = [jnp.sum(total[:, block + n * HEAD : block + (n + 1) * HEAD], axis=1) for n in range(3)]
        factor = row_factor(sums[0], old_width, sums[1])
        inverse_rms = lax.rsqrt(sums[2] * jnp.square(factor) / D_NEW + TOKEN_EPSILON)
        shrunk = (total[:, :block] * (factor * inverse_rms)[:, None]).astype(jnp.bfloat16)
        got["shrunk"] = lax.all_gather(shrunk, "tensor", axis=0, tiled=True)

    shift(0)
    shift(1)
    tokens_share()
    shift(2, 0)
    tokens_share_rest(*arrived(1))
    got["own", 3] = jnp.concatenate([got["own", 3], got["share"]], axis=0)
    shift(3, 1)
    embed(0, 2, ("own", 3))
    inner("q", ("squares", 0))
    ready([("own", "q")], *arrived(3))
    shift("q", 2)
    embed(1, 3, ("own", "q"))
    shift(None, 3)
    embed(2, "q", ("squares", 1))
    shift(None, "q")
    far_q = ("far", "q")
    embed(3, ("far", 3), ("squares", 2), *arrived(far_q), tokens=token_ids.shape[0] // 8)
    tokens_y()
    ready([("old", "k0")], ("squares", 3))
    inner("k0")
    shift("k0")
    ready([("own", "q")], ("own", "k0"))
    places = copies("q", far_q)
    places = [places[:1], places[1:2], places[2:3], places[3:]]
    got["grown", "q"] = grow_projection(order, [(n, 0, found) for n, found in enumerate(places)], expand_in)
    ready([*arrived("k0")], ("grown", "q"))
    shift(None, "k0")
    tokens_x(*arrived("k0"))
    sum_rows(*arrived("k0"))
    tokens_all()
    inner("k1", ("grown", "q"))
    with jax.named_scope("near_k1"):
        near_k1 = [got["own", "k1"], *(permute_dp(got["own", "k1"], flip) for flip in (1, 2, 3))]
    terms = [
        token_term("q", 0, block),
        token_term("k0", 0, KEY_SPLIT) + token_term("k1", KEY_SPLIT, block),
    ]
    far_k0 = ("far", "k0")
    with jax.named_scope("scatter"):
        scattered = scatter_tokens(after(jnp.concatenate(terms, axis=1), *arrived(far_k0)))
    rescale()
    places = copies("k0", far_k0)
    grown_key = grow_projection(
        order, [(n, 0, places[n : n + 1]) for n in range(3)], expand_in, dtype=jnp.float32
    )
    last_terms = [(n, KEY_SPLIT, [(array, 0, head_cols)]) for n, array in enumerate(near_k1)]
    grown_key = grow_projection(order, [*last_terms, (3, 0, places[3:])], expand_in, grown_key)
    attention_entropy = entropy_of(scattered[:, :head_cols], scattered[:, head_cols:], head_count)
    return embedding[0], got["grown", "q"], grown_key, attention_entropy


def solution(mesh):
    placed = (
        P(),
        P("tensor", "dp"),
        P("dp", None),
        P("tensor", None),
        P("tensor", None),
        P("dp", "tensor"),
        P("dp", "tensor"),
    )
    return jax.shard_map(
        ring_plan if (mesh.shape["dp"], mesh.shape["tensor"]) == (4, 8) else plain_plan,
        mesh=mesh,
        in_specs=placed,
        out_specs=(P("tensor", "dp"), P("dp", "tensor"), P("dp", "tensor"), P("dp", "tensor")),
        check_vma=False,
    )
```
